256 devices in a mesh: row: 8 (over z), col: 16 (over y, x_lo, core), layer: 2 (over x_hi).
Axes of the slice: x: 4 (x_hi: 2, x_lo: 2; x = x_hi * 2 + x_lo), y: 4, z: 8, core: 2. Of those that a mesh axis runs over, the one named last changes fastest.
Arguments:
- slab_blocks: float32 [8, 16, 2, 16, 128, 128], P('row', 'col', 'layer'), may hold values from -0.5 to 0.5
- factor_blocks: float32 [8, 16, 2, 16, 1, 128, 128], P('row', 'col', 'layer'), may hold values from -6 to 6
- stack_left: int32 [8, 16, 2, 512], P('row', 'col', 'layer'), may hold values from 0 to 255
- stack_right: int32 [8, 16, 2, 512], P('row', 'col', 'layer'), may hold values from 0 to 127
- stack_target: int32 [8, 16, 2, 512], P('row', 'col', 'layer'), may hold values from 0 to 31
- stack_counts: int32 [8, 16, 2], P('row', 'col', 'layer'), may hold values from 1 to 512, as said below
Outputs:
- product_blocks: float32 [8, 16, 2, 16, 128, 128], P('row', 'col', 'layer')
The draws below stay inside these ranges and needn't reach their ends.
Inputs may be any that keep to these rules, and one draw needn't show every extreme that they name: `stack_counts`: at most 512 listed products on one device; some device lists exactly 512 in every draw. Entries of a list beyond its count are not used.
All inputs are finite; a program needn't handle non-finite values.
Results may differ from the reference program's by a relative error of at most 0.0003.
Values sent between devices are 32-bit elements; how exact they have to be, the bound alone decides.
No kernel may reach another device: no remote copies, remote signals or barrier semaphores. Data moves between devices by JAX's collectives and lax.ppermute only.
A program may use at most 128 MiB of HBM per device.

```python
import jax
import jax.numpy as jnp
from jax import lax

BS = 128
SA = 16
CAPT = 1
PCAP = 512
SCH = 16
N_ROW = 8
N_COL = 16
N_LAYER = 2


def draw_stack_counts(key, part):
    key = jax.random.fold_in(key, 7)
    first_key, second_key = jax.random.split(key)
    every = N_ROW * N_COL * N_LAYER
    raw_draw = jax.random.randint(first_key, (every,), 0, PCAP)
    skewed = raw_draw * raw_draw // PCAP + 1
    chosen = jax.random.randint(second_key, (), 0, every)
    filled = jnp.where(jnp.arange(every, dtype=jnp.int32) == chosen, PCAP, skewed)
    return filled.reshape(N_ROW, N_COL, N_LAYER).astype(jnp.int32)


def place_ends(entries, own_key, least, high):
    spot = [jax.random.randint(jax.random.fold_in(own_key, axis), (), 0, length) for axis, length in enumerate(entries.shape)]
    longest = entries.shape.index(max(entries.shape))
    beside = spot[:longest] + [(spot[longest] + 1) % entries.shape[longest]] + spot[longest + 1:]
    return entries.at[tuple(spot)].set(least).at[tuple(beside)].set(high)


def levels(rng, extent, pieces, low, largest):
    factor_of = 1.0
    for position, shards_of in pieces:
        steps = jax.random.uniform(jax.random.fold_in(jax.random.fold_in(rng, 6), position), (shards_of,), jnp.float32, low / len(pieces), largest / len(pieces))
        factor_of = factor_of * jnp.repeat(jnp.exp(steps), extent[position] // shards_of).reshape((-1,) + (1,) * (len(extent) - 1 - position))
    return factor_of


def noise(own_key, shape, width, bound, pieces=(), held_as=jnp.bfloat16):
    values = width * jax.random.normal(own_key, shape, jnp.float32)
    if pieces:
        values = values * levels(own_key, shape, pieces, -0.22, 0.18)
    return jnp.clip(values, -bound, bound).astype(held_as)


def setup_inputs(seed: int = 0) -> dict:
    seeds = jax.random.split(jax.random.key(seed), 7)
    return {
        "slab_blocks": noise(seeds[0], (N_ROW, N_COL, N_LAYER, SA, BS, BS), BS ** -0.5, 0.5, ((0, 8), (1, 16), (2, 2)), jnp.float32),
        "factor_blocks": noise(seeds[1], (N_ROW, N_COL, N_LAYER, N_COL, CAPT, BS, BS), 1.0, 6.0, ((0, 8), (1, 16), (2, 2)), jnp.float32),
        "stack_left": place_ends(jax.random.randint(seeds[2], (N_ROW, N_COL, N_LAYER, PCAP), 0, N_COL * SA), jax.random.fold_in(seeds[2], 1), 0, (N_COL * SA) - 1).astype(jnp.int32),
        "stack_right": place_ends(jax.random.randint(seeds[3], (N_ROW, N_COL, N_LAYER, PCAP), 0, N_ROW * N_COL * CAPT), jax.random.fold_in(seeds[3], 1), 0, (N_ROW * N_COL * CAPT) - 1).astype(jnp.int32),
        "stack_target": place_ends(jax.random.randint(seeds[4], (N_ROW, N_COL, N_LAYER, PCAP), 0, N_LAYER * SCH), jax.random.fold_in(seeds[4], 1), 0, (N_LAYER * SCH) - 1).astype(jnp.int32),
        "stack_counts": draw_stack_counts(jax.random.fold_in(seeds[6], 71), 0),
    }


def reference(slab_blocks, factor_blocks, stack_left, stack_right, stack_target, stack_counts):
    def one_owner(flat_id):
        row_id = flat_id // N_COL
        col_id = flat_id % N_COL
        running = jnp.zeros((N_LAYER * SCH, BS, BS), jnp.float32)
        for layer_id in range(N_LAYER):
            take_left = stack_left[row_id, col_id, layer_id]
            take_right = stack_right[row_id, col_id, layer_id]
            take_target = stack_target[row_id, col_id, layer_id]
            left_blocks = slab_blocks[row_id, take_left // SA, layer_id, take_left % SA]
            right_blocks = factor_blocks[take_right // (N_COL * CAPT), (take_right // CAPT) % N_COL, layer_id, col_id, take_right % CAPT]
            products = jnp.einsum("pij,pkj->pik", left_blocks, right_blocks, precision=lax.Precision.HIGHEST)
            live_rows = jnp.arange(PCAP, dtype=jnp.int32) < stack_counts[row_id, col_id, layer_id]
            products = jnp.where(live_rows[:, None, None], products, jnp.zeros_like(products))
            running = running + jax.ops.segment_sum(products, take_target, num_segments=N_LAYER * SCH)
        return running.reshape(N_LAYER, SCH, BS, BS)

    result = lax.map(one_owner, jnp.arange(N_ROW * N_COL, dtype=jnp.int32))
    return result.reshape(N_ROW, N_COL, N_LAYER, SCH, BS, BS)
```

```python
import jax
import jax.numpy as jnp
from jax import lax
from jax.experimental import pallas as pl
from jax.experimental.pallas import tpu as pltpu
from jax.sharding import Mesh
from jax.sharding import PartitionSpec as P

BS = 128
SA = 16
SCH = 16
N_ROW = 8
UNROLL = 4
TRANSPOSED = (((1,), (1,)), ((), ()))


def split(block):
    high = block.astype(jnp.bfloat16)
    low = (block - high.astype(jnp.float32)).astype(jnp.bfloat16)
    return high, low


def block_product(left, right):
    left_high, left_low = split(left)
    right_high, right_low = split(right)
    lhs = jnp.concatenate([left_high, left_high, left_low], axis=1)
    rhs = jnp.concatenate([right_high, right_low, right_high], axis=1)
    return lax.dot_general(lhs, rhs, TRANSPOSED, preferred_element_type=jnp.float32)


def multiply_kernel(where, left_index, right_index, target_index, left_own, left_other, *rest):
    pieces, (keep, send, left, right, total, load, store) = rest[:9], rest[9:]
    count, row, core, layer = where[0], where[1], where[2], where[3]
    half = left_own.shape[0]
    copies = [
        pltpu.make_async_copy(left_own, left.at[pl.ds(core * half, half)], load.at[0]),
        pltpu.make_async_copy(left_other, left.at[pl.ds((1 - core) * half, half)], load.at[1]),
    ]
    plan = [(0, 0, 16), (7, 0, 16), (1, 0, 16), (6, 0, 16), (2, 0, 16), (5, 0, 16), (3, 0, 16), (4, 0, 8), (4, 8, 8)]
    for position, (piece, (shift, first, length)) in enumerate(zip(pieces, plan)):
        start = lax.rem(row + shift, N_ROW) * SA + first
        copies.append(pltpu.make_async_copy(piece, right.at[pl.ds(start, length)], load.at[2 + position]))
    for copy in copies:
        copy.start()
    total[...] = jnp.zeros_like(total)
    for copy in copies:
        copy.wait()

    def accumulate(turn, carry):
        products, targets = [], []
        for step in range(UNROLL):
            p = turn * UNROLL + step
            live = p < count
            a = jnp.where(live, left_index[p], 0)
            b = jnp.where(live, right_index[p], 0)
            m = jnp.where(live, target_index[p], 0)
            column = a // SA
            place = lax.rem(column, 2) * half + (column // 2) * SA + lax.rem(a, SA)
            targets.append(jnp.where(live, lax.rem(m // SCH + layer, 2) * SCH + lax.rem(m, SCH), 2 * SCH))
            products.append(block_product(left[place], right[b]))
        for target, product in zip(targets, products):
            total[target] = total[target] + product
        return carry

    lax.fori_loop(0, (count + UNROLL - 1) // UNROLL, accumulate, 0)
    out_send = pltpu.make_async_copy(total.at[pl.ds(SCH, SCH)], send, store.at[0])
    out_keep = pltpu.make_async_copy(total.at[pl.ds(0, SCH)], keep, store.at[1])
    out_send.start()
    out_keep.start()
    out_send.wait()
    out_keep.wait()


def multiply(where, left_index, right_index, target_index, left_own, left_other, pieces):
    block = jax.ShapeDtypeStruct((SCH, BS, BS), jnp.float32)
    scalars = pl.BlockSpec(memory_space=pltpu.SMEM)
    whole = pl.BlockSpec(memory_space=pl.ANY)
    return pl.pallas_call(
        multiply_kernel,
        out_shape=(block, block),
        in_specs=[scalars] * 4 + [whole] * (2 + len(pieces)),
        out_specs=(whole, whole),
        scratch_shapes=[
            pltpu.VMEM((256, BS, BS), jnp.float32),
            pltpu.VMEM((128, BS, BS), jnp.float32),
            pltpu.VMEM((2 * SCH + 1, BS, BS), jnp.float32),
            pltpu.SemaphoreType.DMA((2 + len(pieces),)),
            pltpu.SemaphoreType.DMA((2,)),
        ],
        compiler_params=pltpu.CompilerParams(vmem_limit_bytes=40 << 20),
        cost_estimate=pl.CostEstimate(flops=512 * 6 * BS**3, bytes_accessed=26 << 20, transcendentals=0),
        name="multiply",
    )(where, left_index, right_index, target_index, left_own, left_other, *pieces)


def shift(value, axis, by):
    size = lax.axis_size(axis)
    return lax.ppermute(value, axis, [(i, (i + by) % size) for i in range(size)])


def body(slab_blocks, factor_blocks, stack_left, stack_right, stack_target, stack_counts):
    slab = slab_blocks.reshape(SA, BS, BS)
    left_own = lax.all_gather(slab, ("y", "x"), axis=0, tiled=True)
    left_other = shift(left_own, "core", 1)

    mine = lax.all_to_all(factor_blocks.reshape(SA, BS, BS), ("y", "x", "core"), split_axis=0, concat_axis=0, tiled=True)
    up = down = mine
    pieces = [mine]
    for _ in range(3):
        up, down = shift(up, "row", 1), shift(down, "row", -1)
        pieces += [up, down]
    pieces += [shift(up[:8], "row", 1), shift(down[8:], "row", -1)]

    where = jnp.stack(
        [stack_counts.reshape(()), lax.axis_index("row"), lax.axis_index("core"), lax.axis_index("layer")]
    ).astype(jnp.int32)
    keep, send = multiply(
        where,
        stack_left.reshape(-1),
        stack_right.reshape(-1),
        stack_target.reshape(-1),
        left_own,
        left_other,
        pieces,
    )
    summed = keep + shift(send, "layer", 1)
    return summed.reshape((1, 1, 1) + summed.shape)


def solution(mesh):
    fine = Mesh(mesh.devices.reshape(8, 4, 2, 2, 2), ("row", "y", "x", "core", "layer"))
    col = ("y", "x", "core")
    return jax.shard_map(
        body,
        mesh=fine,
        in_specs=(
            P("row", col, "layer", None, None, None),
            P("row", col, "layer", None, None, None, None),
            P("row", col, "layer", None),
            P("row", col, "layer", None),
            P("row", col, "layer", None),
            P("row", col, "layer"),
        ),
        out_specs=P("row", col, "layer", None, None, None),
        check_vma=False,
    )
```

```python
import jax
import jax.numpy as jnp
from jax import lax
from jax.experimental import pallas as pl
from jax.experimental.pallas import tpu as pltpu
from jax.sharding import Mesh
from jax.sharding import PartitionSpec as P

BS = 128
SA = 16
SCH = 16
N_ROW = 8
N_LEFT = 256
N_RIGHT = 128
PCAP = 512
UNROLL = 16
BINS = 5
LISTED = PCAP + BINS * UNROLL
SPARE = 2 * SCH
TRANSPOSED = (((1,), (1,)), ((), ()))

SCALARS = pl.BlockSpec(memory_space=pltpu.SMEM)
IN_HBM = pl.BlockSpec(memory_space=pltpu.HBM)
VMEM = pl.BlockSpec(memory_space=pltpu.VMEM)
TOKEN = jax.ShapeDtypeStruct((1,), jnp.int32)
STATE = (
    pltpu.VMEM((N_LEFT, BS, BS), jnp.float32),
    pltpu.VMEM((N_RIGHT, BS, BS), jnp.float32),
    pltpu.VMEM((2 * SCH + 1, BS, BS), jnp.float32),
)


def hbm(*arrays):
    return [pltpu.with_memory_space_constraint(a, pltpu.HBM) for a in arrays]


def split(block):
    high = block.astype(jnp.bfloat16)
    low = (block - high.astype(jnp.float32)).astype(jnp.bfloat16)
    return high, low


def block_product(left, right):
    left_high, left_low = split(left)
    right_high, right_low = split(right)
    lhs = jnp.concatenate([left_high, left_high, left_low], axis=1)
    rhs = jnp.concatenate([right_high, right_low, right_high], axis=1)
    return lax.dot_general(lhs, rhs, TRANSPOSED, preferred_element_type=jnp.float32)


def stage_kernel(bins, sides, first, base, starts, bounds, listed, *refs):
    pieces, refs = refs[: len(sides)], refs[len(sides) :]
    if not first:
        refs = refs[3:]
    left, right, total, done = refs[:4]
    sems = refs[-1]
    copies = []
    for piece, (side, parts) in zip(pieces, sides):
        length = piece.shape[0] // parts
        for part in range(parts):
            i = len(copies)
            source = piece.at[pl.ds(part * length, length)]
            copies.append(pltpu.make_async_copy(source, (left, right)[side].at[pl.ds(starts[base + i], length)], sems.at[i]))
    for copy in copies:
        copy.start()
    if first:
        total[...] = jnp.zeros_like(total)
    for copy in copies:
        copy.wait()

    def accumulate(turn, carry):
        products, targets = [], []
        for step in range(UNROLL):
            code = listed[turn * UNROLL + step]
            targets.append(code & 255)
            products.append(block_product(left[code >> 16], right[(code >> 8) & 255]))
        for target, product in zip(targets, products):
            total[target] = total[target] + product
        return carry

    lax.fori_loop(bounds[bins[0]], bounds[bins[1]], accumulate, 0)
    done[0] = bounds[0]


def stage(bins, base, lefts, rights, bounds, listed, starts, state=None, flops=0):
    pieces = lefts + rights
    sides = [(int(i >= len(lefts)), n) for i, (n, _) in enumerate(pieces)]
    aliases = {} if state is None else {3 + len(pieces) + i: i for i in range(3)}
    *state, token = pl.pallas_call(
        lambda *refs: stage_kernel(bins, sides, not aliases, base, *refs),
        out_shape=[*STATE, TOKEN],
        in_specs=[SCALARS] * 3 + [IN_HBM] * len(pieces) + [VMEM] * len(aliases),
        out_specs=[VMEM] * 3 + [SCALARS],
        input_output_aliases=aliases,
        scratch_shapes=[pltpu.SemaphoreType.DMA((max(1, sum(n for _, n in sides)),))],
        compiler_params=pltpu.CompilerParams(vmem_limit_bytes=8 << 20),
        cost_estimate=pl.CostEstimate(flops=flops, bytes_accessed=0, transcendentals=0),
        name="stage_" + "_".join(map(str, bins)),
    )(starts, bounds, listed, *hbm(*[a for _, a in pieces]), *(state or ()))
    return state, token


def tie_kernel(*refs):
    token, scratch = refs[-2:]
    scratch[...] = jnp.zeros_like(scratch)
    token[0] = 0


def tie(arrays, tokens=()):
    *arrays, token = pl.pallas_call(
        tie_kernel,
        out_shape=[pltpu.HBM(a.shape, a.dtype) for a in arrays] + [TOKEN],
        in_specs=[IN_HBM] * len(arrays) + [SCALARS] * len(tokens),
        out_specs=[IN_HBM] * len(arrays) + [SCALARS],
        input_output_aliases={i: i for i in range(len(arrays))},
        scratch_shapes=[pltpu.VMEM((8, BS), jnp.float32)],
        compiler_params=pltpu.CompilerParams(vmem_limit_bytes=1 << 20),
        cost_estimate=pl.CostEstimate(flops=0, bytes_accessed=0, transcendentals=0),
        name="tie",
    )(*hbm(*arrays), *tokens)
    return arrays, token


def pack_kernel(n, *refs):
    pieces, (out, bounce, into, leave) = refs[:n], refs[-4:]
    slots = [pl.ds(i * SA, SA) for i in range(n)]
    fill = [pltpu.make_async_copy(piece, bounce.at[rows], into.at[i]) for i, (piece, rows) in enumerate(zip(pieces, slots))]
    drain = [pltpu.make_async_copy(bounce.at[rows], out.at[rows], leave.at[i]) for i, rows in enumerate(slots)]
    for copy in fill:
        copy.start()
    for first, second in zip(fill, drain):
        first.wait()
        second.start()
    for copy in drain:
        copy.wait()


def pack(*pieces, later_than=()):
    n = len(pieces)
    return pl.pallas_call(
        lambda *refs: pack_kernel(n, *refs),
        out_shape=pltpu.HBM((n * SA, BS, BS), jnp.float32),
        in_specs=[IN_HBM] * (n + len(later_than)),
        out_specs=IN_HBM,
        scratch_shapes=[
            pltpu.VMEM((n * SA, BS, BS), jnp.float32),
            pltpu.SemaphoreType.DMA((n,)),
            pltpu.SemaphoreType.DMA((n,)),
        ],
        compiler_params=pltpu.CompilerParams(vmem_limit_bytes=(n + 1) << 20),
        cost_estimate=pl.CostEstimate(flops=0, bytes_accessed=0, transcendentals=0),
        name="pack",
    )(*hbm(*pieces, *later_than))


def halves_kernel(up, down, up_half, down_half, sems):
    copies = [
        pltpu.make_async_copy(up.at[pl.ds(0, SA // 2)], up_half, sems.at[0]),
        pltpu.make_async_copy(down.at[pl.ds(SA // 2, SA // 2)], down_half, sems.at[1]),
    ]
    for copy in copies:
        copy.start()
    for copy in copies:
        copy.wait()


def halves(up, down):
    half = pltpu.VMEM((SA // 2, BS, BS), jnp.float32)
    return pl.pallas_call(
        halves_kernel,
        out_shape=(half, half),
        in_specs=[IN_HBM] * 2,
        out_specs=(VMEM, VMEM),
        scratch_shapes=[pltpu.SemaphoreType.DMA((2,))],
        compiler_params=pltpu.CompilerParams(vmem_limit_bytes=1 << 20),
        cost_estimate=pl.CostEstimate(flops=0, bytes_accessed=0, transcendentals=0),
        name="halves",
    )(*hbm(up, down))


def shift(value, axis, by):
    size = lax.axis_size(axis)
    return lax.ppermute(value, axis, [(i, (i + by) % size) for i in range(size)])


def order(left_index, right_index, target_index, count, row, layer, left_class):
    p = jnp.arange(PCAP, dtype=jnp.int32)
    away = (right_index // SA - row) % N_ROW
    kept = target_index // SCH == layer
    right_class = jnp.where((away <= 2) | (away >= 6), 0, jnp.where(away == 4, 2, 1))
    here = jnp.maximum(left_class, right_class)
    bins = jnp.where(here == 0, jnp.where(kept, 1, 0), jnp.where(kept, 4, 1 + here))
    bins = jnp.where(p < count, bins, BINS)
    target = jnp.where(kept, 0, SCH) + target_index % SCH
    code = (left_index << 16) | (right_index << 8) | target
    same = bins[:, None] == bins[None, :]
    rank = jnp.sum(same & (p[None, :] < p[:, None]), axis=1, dtype=jnp.int32)
    held = jnp.sum(bins[None, :] == jnp.arange(BINS, dtype=jnp.int32)[:, None], axis=1, dtype=jnp.int32)
    groups = (held + UNROLL - 1) // UNROLL
    b = jnp.arange(BINS + 1, dtype=jnp.int32)
    bounds = jnp.sum(jnp.where(b[None, :BINS] < b[:, None], groups[None, :], 0), axis=1, dtype=jnp.int32)
    start = jnp.sum(jnp.where(bins[:, None] == b[None, :BINS], bounds[None, :BINS] * UNROLL, 0), axis=1)
    place = jnp.where(bins < BINS, start + rank, -1)
    slot = jnp.arange(LISTED, dtype=jnp.int32)
    hit = place[None, :] == slot[:, None]
    listed = SPARE + jnp.sum(jnp.where(hit, code[None, :] - SPARE, 0), axis=1, dtype=jnp.int32)
    return bounds, listed


def body(slab_blocks, factor_blocks, stack_left, stack_right, stack_target, stack_counts):
    row, layer = lax.axis_index("row"), lax.axis_index("layer")
    y, x, core = lax.axis_index("y"), lax.axis_index("x"), lax.axis_index("core")

    left_index = stack_left.reshape(-1)
    across_y = (left_index // (4 * SA) - y) % 4
    across_x = (left_index // (2 * SA) - x) % 2
    left_class = jnp.where(across_y == 2, jnp.where(across_x == 0, 1, 2), jnp.where((across_y != 0) & (across_x == 1), 2, 0))
    bounds, listed = order(
        left_index,
        stack_right.reshape(-1),
        stack_target.reshape(-1),
        stack_counts.reshape(()),
        row,
        layer,
        left_class,
    )

    def left_at(dy, dx, dc, first=0):
        return (((y + dy) % 4 * 2 + (x + dx) % 2) * 2 + (core + dc) % 2) * SA + first

    def right_at(away, first=0):
        return (row + away) % N_ROW * SA + first

    own = slab_blocks.reshape(SA, BS, BS)
    mine = lax.all_to_all(factor_blocks.reshape(SA, BS, BS), ("y", "x", "core"), split_axis=0, concat_axis=0, tiled=True)

    first_places = [left_at(0, 0, 0), left_at(0, 0, 1), left_at(-1, 0, 0), left_at(1, 0, 0), left_at(0, 1, 0)]
    first_places += [left_at(-1, 0, 1), left_at(1, 0, 1), left_at(0, 1, 1)]
    first_places += [right_at(away) for away in (0, -1, 1, -2, 2)]
    second_places = [left_at(2, 0, 0), left_at(2, 0, 1), right_at(-3), right_at(3)]
    third_places = [left_at(dy, 1, dc) for dy in (1, -1, 2) for dc in range(2)] + [right_at(4), right_at(4, 8)]
    starts = jnp.stack(first_places + second_places + third_places)
    second, third = len(first_places), len(first_places) + len(second_places)

    up1, down1 = shift(mine, "row", 1), shift(mine, "row", -1)
    own_c = shift(own, "core", 1)
    sent = pack(own, later_than=(own_c,))
    own_up, own_down, across = shift(sent, "y", 1), shift(sent, "y", -1), shift(sent, "x", 1)
    packed = pack(own_up, own_down, across)
    (up1, down1, own_up, own_down, across, own_c, packed), t1 = tie((up1, down1, own_up, own_down, across, own_c, packed))

    up2, down2 = shift(up1, "row", 1), shift(down1, "row", -1)
    own_far, across_down = shift(own_up, "y", 1), shift(across, "y", -1)
    packed_c = shift(packed, "core", 1)
    (up2, down2, own_far, across_down, packed_c), t2 = tie((up2, down2, own_far, across_down, packed_c), (t1,))

    up3, down3 = shift(up2, "row", 1), shift(down2, "row", -1)
    far, across_up = shift(across_down, "y", -1), shift(own_up, "x", 1)
    own_far_c = shift(own_far, "core", 1)
    lefts = [(1, own), (1, own_c), (1, own_up), (1, own_down), (1, across), (3, packed_c)]
    rights = [(1, mine), (1, up1), (1, down1), (1, up2), (1, down2)]
    state, done = stage((0, 2), 0, lefts, rights, bounds, listed, starts, flops=8 * 10**9)
    (up3, down3, far, across_up, own_far_c), t3 = tie((up3, down3, far, across_up, own_far_c), (t2, done))

    up3_half, down3_half = halves(up3, down3)
    up4, down4 = shift(up3_half, "row", 1), shift(down3_half, "row", -1)
    across_down_c, across_up_c, far_c = shift(across_down, "core", 1), shift(across_up, "core", 1), shift(far, "core", 1)
    lefts, rights = [(1, own_far), (1, own_far_c)], [(1, up3), (1, down3)]
    state, done = stage((2, 3), second, lefts, rights, bounds, listed, starts, state, flops=4 * 10**9)
    (up4, down4, across_down_c, across_up_c, far_c), t4 = tie((up4, down4, across_down_c, across_up_c, far_c), (t3, done))

    lefts = [(1, a) for a in (across_down, across_down_c, across_up, across_up_c, far, far_c)]
    state, _ = stage((3, 4), third, lefts, [(1, up4), (1, down4)], bounds, listed, starts, state)
    arrived = shift(state[2][SCH : 2 * SCH], "layer", 1)
    state, _ = stage((4, 5), 0, [], [], bounds, listed, starts, state, flops=10**10)
    summed = state[2][:SCH] + arrived
    return summed.reshape((1, 1, 1) + summed.shape)


def solution(mesh):
    fine = Mesh(mesh.devices.reshape(8, 4, 2, 2, 2), ("row", "y", "x", "core", "layer"))
    col = ("y", "x", "core")
    return jax.shard_map(
        body,
        mesh=fine,
        in_specs=(
            P("row", col, "layer", None, None, None),
            P("row", col, "layer", None, None, None, None),
            P("row", col, "layer", None),
            P("row", col, "layer", None),
            P("row", col, "layer", None),
            P("row", col, "layer"),
        ),
        out_specs=P("row", col, "layer", None, None, None),
        check_vma=False,
    )
```

```python
import jax
import jax.numpy as jnp
from jax import lax
from jax.experimental import pallas as pl
from jax.experimental.pallas import tpu as pltpu
from jax.sharding import Mesh
from jax.sharding import PartitionSpec as P

BS = 128
SA = 16
SCH = 16
N_ROW = 8
N_LEFT = 256
N_RIGHT = 128
PCAP = 512
UNROLL = 16
BINS = 6
LISTED = PCAP + BINS * UNROLL
SPARE = 2 * SCH

SCALARS = pl.BlockSpec(memory_space=pltpu.SMEM)
IN_HBM = pl.BlockSpec(memory_space=pltpu.HBM)
ANYWHERE = pl.BlockSpec(memory_space=pl.ANY)
VMEM = pl.BlockSpec(memory_space=pltpu.VMEM)
TOKEN = jax.ShapeDtypeStruct((1,), jnp.int32)
STATE = (
    pltpu.VMEM((N_LEFT, BS, BS), jnp.float32),
    pltpu.VMEM((N_RIGHT, BS, 2 * BS), jnp.bfloat16),
    pltpu.VMEM((2 * SCH + 1, BS, BS), jnp.float32),
)


def hbm(*arrays):
    return [pltpu.with_memory_space_constraint(a, pltpu.HBM) for a in arrays]


def vmem(*arrays):
    return [pltpu.with_memory_space_constraint(a, pltpu.VMEM) for a in arrays]


def split(block):
    high = block.astype(jnp.bfloat16)
    low = (block - high.astype(jnp.float32)).astype(jnp.bfloat16)
    return high, low


def block_product(left, right):
    lhs = jnp.concatenate(split(left), axis=1)
    rhs = jnp.concatenate([right, right], axis=0)
    both = lax.dot_general(lhs, rhs, (((1,), (0,)), ((), ())), preferred_element_type=jnp.float32)
    return both[:, :BS] + both[:, BS:]


def stage_kernel(bins, parts, n_rights, first, base, starts, bounds, listed, *refs):
    lefts, rights, refs = refs[: len(parts)], refs[len(parts) : len(parts) + n_rights], refs[len(parts) + n_rights :]
    if not first:
        refs = refs[3:]
    left, right, total, done, sems = refs
    copies = []
    for piece, n in zip(lefts, parts):
        length = piece.shape[0] // n
        for part in range(n):
            i = len(copies)
            source = piece.at[pl.ds(part * length, length)]
            copies.append(pltpu.make_async_copy(source, left.at[pl.ds(starts[base + i], length)], sems.at[i]))
    for copy in copies:
        copy.start()
    if first:
        total[...] = jnp.zeros_like(total)
    for i, piece in enumerate(rights):
        place = starts[base + len(copies) + i]

        def prepare(turn, carry, piece=piece, place=place):
            for step in range(8):
                block = turn * 8 + step
                high, low = split(piece[block])
                right[place + block, :, :BS] = high.T
                right[place + block, :, BS:] = low.T
            return carry

        lax.fori_loop(0, piece.shape[0] // 8, prepare, 0)
    for copy in copies:
        copy.wait()

    def accumulate(turn, carry):
        products, targets = [], []
        for step in range(UNROLL):
            code = listed[turn * UNROLL + step]
            targets.append(code & 255)
            products.append(block_product(left[code >> 16], right[(code >> 8) & 255]))
        for target, product in zip(targets, products):
            total[target] = total[target] + product
        return carry

    lax.fori_loop(bounds[bins[0]], bounds[bins[1]], accumulate, 0)
    done[0] = bounds[0]


def stage(bins, base, lefts, rights, bounds, listed, starts, state=None, flops=0, place=IN_HBM, tokens=()):
    parts, pieces = [n for n, _ in lefts], [a for _, a in lefts]
    n = len(tokens) + 3 + len(lefts) + len(rights)
    aliases = {} if state is None else {n + i: i for i in range(3)}
    *state, token = pl.pallas_call(
        lambda *refs: stage_kernel(bins, parts, len(rights), not aliases, base, *refs[len(tokens) :]),
        out_shape=[*STATE, TOKEN],
        in_specs=[SCALARS] * (len(tokens) + 3) + [place] * len(lefts) + [VMEM] * (len(rights) + len(aliases)),
        out_specs=[VMEM] * 3 + [SCALARS],
        input_output_aliases=aliases,
        scratch_shapes=[pltpu.SemaphoreType.DMA((max(1, sum(parts)),))],
        compiler_params=pltpu.CompilerParams(vmem_limit_bytes=10 << 20),
        cost_estimate=pl.CostEstimate(flops=flops, bytes_accessed=0, transcendentals=0),
        name="stage_" + "_".join(map(str, bins)),
    )(*tokens, starts, bounds, listed, *(hbm(*pieces) if place is IN_HBM else pieces), *vmem(*rights), *(state or ()))
    return state, token


def tie_kernel(*refs):
    token, scratch = refs[-2:]
    scratch[...] = jnp.zeros_like(scratch)
    token[0] = 0


def tie(arrays, tokens=(), place=ANYWHERE):
    shape = jax.ShapeDtypeStruct if place is ANYWHERE else pltpu.HBM
    *arrays, token = pl.pallas_call(
        tie_kernel,
        out_shape=[shape(a.shape, a.dtype) for a in arrays] + [TOKEN],
        in_specs=[place] * len(arrays) + [SCALARS] * len(tokens),
        out_specs=[place] * len(arrays) + [SCALARS],
        input_output_aliases={i: i for i in range(len(arrays))},
        scratch_shapes=[pltpu.VMEM((8, BS), jnp.float32)],
        compiler_params=pltpu.CompilerParams(vmem_limit_bytes=1 << 20),
        cost_estimate=pl.CostEstimate(flops=0, bytes_accessed=0, transcendentals=0),
        name="tie",
    )(*(arrays if place is ANYWHERE else hbm(*arrays)), *tokens)
    return arrays, token


def witness(arrays, tokens=()):
    return pl.pallas_call(
        tie_kernel,
        out_shape=TOKEN,
        in_specs=[ANYWHERE] * len(arrays) + [SCALARS] * len(tokens),
        out_specs=SCALARS,
        scratch_shapes=[pltpu.VMEM((8, BS), jnp.float32)],
        compiler_params=pltpu.CompilerParams(vmem_limit_bytes=1 << 20),
        cost_estimate=pl.CostEstimate(flops=0, bytes_accessed=0, transcendentals=0),
        name="witness",
    )(*arrays, *tokens)


def pack_kernel(n, *refs):
    pieces, (out, bounce, into, leave) = refs[:n], refs[-4:]
    slots = [pl.ds(i * SA, SA) for i in range(n)]
    fill = [pltpu.make_async_copy(piece, bounce.at[rows], into.at[i]) for i, (piece, rows) in enumerate(zip(pieces, slots))]
    drain = [pltpu.make_async_copy(bounce.at[rows], out.at[rows], leave.at[i]) for i, rows in enumerate(slots)]
    for copy in fill:
        copy.start()
    for first, second in zip(fill, drain):
        first.wait()
        second.start()
    for copy in drain:
        copy.wait()


def pack(*pieces, later_than=()):
    n = len(pieces)
    return pl.pallas_call(
        lambda *refs: pack_kernel(n, *refs),
        out_shape=pltpu.HBM((n * SA, BS, BS), jnp.float32),
        in_specs=[IN_HBM] * (n + len(later_than)),
        out_specs=IN_HBM,
        scratch_shapes=[
            pltpu.VMEM((n * SA, BS, BS), jnp.float32),
            pltpu.SemaphoreType.DMA((n,)),
            pltpu.SemaphoreType.DMA((n,)),
        ],
        compiler_params=pltpu.CompilerParams(vmem_limit_bytes=(n + 1) << 20),
        cost_estimate=pl.CostEstimate(flops=0, bytes_accessed=0, transcendentals=0),
        name="pack",
    )(*hbm(*pieces, *later_than))


def shift(value, axis, by):
    size = lax.axis_size(axis)
    return lax.ppermute(value, axis, [(i, (i + by) % size) for i in range(size)])


def shift_apart(value, axis):
    size = lax.axis_size(axis)
    pairs = [(2 * i + core, (i + 1 - 2 * core) % size * 2 + core) for i in range(size) for core in range(2)]
    return lax.ppermute(value, (axis, "core"), pairs)


def order(left_index, right_index, target_index, count, row, layer, left_class):
    p = jnp.arange(PCAP, dtype=jnp.int32)
    away = (right_index // SA - row) % N_ROW
    kept = target_index // SCH == layer
    right_class = jnp.where((away <= 2) | (away >= 6), 0, jnp.where(away == 4, 2, 1))
    here = jnp.maximum(left_class, right_class)
    bins = jnp.where(here == 0, jnp.where(kept, 1, 0), jnp.where(kept, 5, 1 + here + (here == 2) * (target_index % SCH // (SCH // 2))))
    bins = jnp.where(p < count, bins, BINS)
    target = jnp.where(kept, 0, SCH) + target_index % SCH
    code = (left_index << 16) | (right_index << 8) | target
    same = bins[:, None] == bins[None, :]
    rank = jnp.sum(same & (p[None, :] < p[:, None]), axis=1, dtype=jnp.int32)
    held = jnp.sum(bins[None, :] == jnp.arange(BINS, dtype=jnp.int32)[:, None], axis=1, dtype=jnp.int32)
    groups = (held + UNROLL - 1) // UNROLL
    b = jnp.arange(BINS + 1, dtype=jnp.int32)
    bounds = jnp.sum(jnp.where(b[None, :BINS] < b[:, None], groups[None, :], 0), axis=1, dtype=jnp.int32)
    start = jnp.sum(jnp.where(bins[:, None] == b[None, :BINS], bounds[None, :BINS] * UNROLL, 0), axis=1)
    place = jnp.where(bins < BINS, start + rank, -1)
    slot = jnp.arange(LISTED, dtype=jnp.int32)
    hit = place[None, :] == slot[:, None]
    listed = SPARE + jnp.sum(jnp.where(hit, code[None, :] - SPARE, 0), axis=1, dtype=jnp.int32)
    return bounds, listed


def body(slab_blocks, factor_blocks, stack_left, stack_right, stack_target, stack_counts):
    row, layer = lax.axis_index("row"), lax.axis_index("layer")
    y, x, core = lax.axis_index("y"), lax.axis_index("x"), lax.axis_index("core")

    left_index = stack_left.reshape(-1)
    across_y = (left_index // (4 * SA) - y) % 4
    across_x = (left_index // (2 * SA) - x) % 2
    left_class = jnp.where(across_x == 0, jnp.where(across_y == 2, 1, 0), jnp.where(across_y < 2, across_y, 2))
    bounds, listed = order(
        left_index,
        stack_right.reshape(-1),
        stack_target.reshape(-1),
        stack_counts.reshape(()),
        row,
        layer,
        left_class,
    )

    def left_at(dy, dx, dc, first=0):
        return (((y + dy) % 4 * 2 + (x + dx) % 2) * 2 + (core + dc) % 2) * SA + first

    def right_at(away, first=0):
        return (row + away) % N_ROW * SA + first

    own = slab_blocks.reshape(SA, BS, BS)
    mine = lax.all_to_all(factor_blocks.reshape(SA, BS, BS), ("y", "x", "core"), split_axis=0, concat_axis=0, tiled=True)

    first_places = [left_at(0, 0, 0), left_at(0, 0, 1), left_at(-1, 0, 0), left_at(1, 0, 0), left_at(0, 1, 0)]
    first_places += [left_at(-1, 0, 1), left_at(1, 0, 1), left_at(0, 1, 1)]
    first_places += [right_at(away) for away in (0, -1, 1, -2, 2)]
    second_places = [left_at(dy, dx, dc) for dy, dx in ((2, 0), (1, 1)) for dc in range(2)] + [right_at(-3), right_at(3)]
    third_places = [left_at(dy, 1, dc) for dy in (-1, 2) for dc in range(2)] + [right_at(4)]
    starts = jnp.stack(first_places + second_places + third_places)
    second, third = len(first_places), len(first_places) + len(second_places)

    up1, down1 = shift(mine, "row", 1), shift(mine, "row", -1)
    own_c = shift(own, "core", 1)
    sent = pack(own, later_than=(shift(own[:1], "core", 1),))
    own_up, own_down, across = shift(sent, "y", 1), shift(sent, "y", -1), shift(sent, "x", 1)
    own_up_c, own_down_c, across_c = shift(own_up, "core", 1), shift(own_down, "core", 1), shift(across, "core", 1)
    z1 = witness((up1, down1))
    (own_up, own_down, across, own_c, own_up_c, own_down_c, across_c), _ = tie(
        (own_up, own_down, across, own_c, own_up_c, own_down_c, across_c), (z1,), IN_HBM
    )

    up2, down2 = shift(up1, "row", 1), shift(down1, "row", -1)
    own_far, across_down, across_up = shift(own_up, "y", 1), shift(across, "y", -1), shift(own_up, "x", 1)
    z2 = witness((up2, down2))
    (own_far, across_down, across_up), t2 = tie((own_far, across_down, across_up), (z2,), IN_HBM)

    up3, down3 = shift(up2, "row", 1), shift(down2, "row", -1)
    far = shift_apart(jnp.where(core == 0, across_up, across_down), "y")
    across_down_c = shift(across_down, "core", 1)
    lefts = [(1, a) for a in (own, own_c, own_up, own_down, across, own_up_c, own_down_c, across_c)]
    state, done = stage((0, 2), 0, lefts, [mine, up1, down1, up2, down2], bounds, listed, starts, flops=8 * 10**9, tokens=(t2,))

    (own_far,), _ = tie((own_far,), (done,), IN_HBM)
    own_far_c = shift(own_far, "core", 1)

    opposite = shift_apart(jnp.where(core == 0, up3, down3), "row")
    far_c, across_up_c = shift(far, "core", 1), shift(across_up, "core", 1)
    lefts = [(1, a) for a in (own_far, own_far_c, across_down, across_down_c)]
    state, done = stage((2, 3), second, lefts, [up3, down3], bounds, listed, starts, state, flops=10**9)

    lefts = [(1, a) for a in (across_up, across_up_c, far, far_c)]
    state, _ = stage((3, 4), third, lefts, [opposite], bounds, listed, starts, state, place=ANYWHERE)
    arrived_low = shift(state[2][SCH : SCH + SCH // 2], "layer", 1)
    state, _ = stage((4, 5), 0, [], [], bounds, listed, starts, state)
    arrived_high = shift(state[2][SCH + SCH // 2 : 2 * SCH], "layer", 1)
    state, _ = stage((5, 6), 0, [], [], bounds, listed, starts, state, flops=10**10)
    summed = state[2][:SCH] + jnp.concatenate([arrived_low, arrived_high])
    return summed.reshape((1, 1, 1) + summed.shape)


def solution(mesh):
    fine = Mesh(mesh.devices.reshape(8, 4, 2, 2, 2), ("row", "y", "x", "core", "layer"))
    col = ("y", "x", "core")
    return jax.shard_map(
        body,
        mesh=fine,
        in_specs=(
            P("row", col, "layer", None, None, None),
            P("row", col, "layer", None, None, None, None),
            P("row", col, "layer", None),
            P("row", col, "layer", None),
            P("row", col, "layer", None),
            P("row", col, "layer"),
        ),
        out_specs=P("row", col, "layer", None, None, None),
        check_vma=False,
    )
```

```python
import jax
import jax.numpy as jnp
from jax import lax
from jax.experimental import pallas as pl
from jax.experimental.pallas import tpu as pltpu
from jax.sharding import Mesh
from jax.sharding import PartitionSpec as P

BS = 128
SA = 16
SCH = 16
N_ROW = 8
N_LEFT = 256
N_RIGHT = 128
PCAP = 512
UNROLL = 16
BINS = 6
LISTED = PCAP + BINS * UNROLL
SPARE = 2 * SCH

SCALARS = pl.BlockSpec(memory_space=pltpu.SMEM)
IN_HBM = pl.BlockSpec(memory_space=pltpu.HBM)
ANYWHERE = pl.BlockSpec(memory_space=pl.ANY)
VMEM = pl.BlockSpec(memory_space=pltpu.VMEM)
TOKEN = jax.ShapeDtypeStruct((1,), jnp.int32)
STATE = (
    pltpu.VMEM((N_LEFT, BS, BS), jnp.float32),
    pltpu.VMEM((N_RIGHT, BS, 2 * BS), jnp.bfloat16),
    pltpu.VMEM((2 * SCH + 1, BS, BS), jnp.float32),
)


def hbm(*arrays):
    return [pltpu.with_memory_space_constraint(a, pltpu.HBM) for a in arrays]


def vmem(*arrays):
    return [pltpu.with_memory_space_constraint(a, pltpu.VMEM) for a in arrays]


def split(block):
    high = block.astype(jnp.bfloat16)
    low = (block - high.astype(jnp.float32)).astype(jnp.bfloat16)
    return high, low


def block_product(left, right):
    lhs = jnp.concatenate(split(left), axis=1)
    rhs = jnp.concatenate([right, right], axis=0)
    both = lax.dot_general(lhs, rhs, (((1,), (0,)), ((), ())), preferred_element_type=jnp.float32)
    return both[:, :BS] + both[:, BS:]


def stage_kernel(bins, parts, n_rights, first, base, starts, bounds, listed, *refs):
    lefts, rights, refs = refs[: len(parts)], refs[len(parts) : len(parts) + n_rights], refs[len(parts) + n_rights :]
    if not first:
        refs = refs[3:]
    left, right, total, done, sems = refs
    copies = []
    for piece, n in zip(lefts, parts):
        length = piece.shape[0] // n
        for part in range(n):
            i = len(copies)
            source = piece.at[pl.ds(part * length, length)]
            copies.append(pltpu.make_async_copy(source, left.at[pl.ds(starts[base + i], length)], sems.at[i]))
    for copy in copies:
        copy.start()
    if first:
        total[...] = jnp.zeros_like(total)
    for i, piece in enumerate(rights):
        place = starts[base + len(copies) + i]

        def prepare(turn, carry, piece=piece, place=place):
            for step in range(8):
                block = turn * 8 + step
                high, low = split(piece[block])
                right[place + block, :, :BS] = high.T
                right[place + block, :, BS:] = low.T
            return carry

        lax.fori_loop(0, piece.shape[0] // 8, prepare, 0)
    for copy in copies:
        copy.wait()

    def accumulate(turn, carry):
        products, targets = [], []
        for step in range(UNROLL):
            code = listed[turn * UNROLL + step]
            targets.append(code & 255)
            products.append(block_product(left[code >> 16], right[(code >> 8) & 255]))
        for target, product in zip(targets, products):
            total[target] = total[target] + product
        return carry

    lax.fori_loop(bounds[bins[0]], bounds[bins[1]], accumulate, 0)
    done[0] = bounds[0]


def stage(bins, base, lefts, rights, bounds, listed, starts, state=None, flops=0, place=IN_HBM, tokens=()):
    parts, pieces = [n for n, _ in lefts], [a for _, a in lefts]
    n = len(tokens) + 3 + len(lefts) + len(rights)
    aliases = {} if state is None else {n + i: i for i in range(3)}
    *state, token = pl.pallas_call(
        lambda *refs: stage_kernel(bins, parts, len(rights), not aliases, base, *refs[len(tokens) :]),
        out_shape=[*STATE, TOKEN],
        in_specs=[SCALARS] * (len(tokens) + 3) + [place] * len(lefts) + [VMEM] * (len(rights) + len(aliases)),
        out_specs=[VMEM] * 3 + [SCALARS],
        input_output_aliases=aliases,
        scratch_shapes=[pltpu.SemaphoreType.DMA((max(1, sum(parts)),))],
        compiler_params=pltpu.CompilerParams(vmem_limit_bytes=10 << 20),
        cost_estimate=pl.CostEstimate(flops=flops, bytes_accessed=0, transcendentals=0),
        name="stage_" + "_".join(map(str, bins)),
    )(*tokens, starts, bounds, listed, *(hbm(*pieces) if place is IN_HBM else pieces), *vmem(*rights), *(state or ()))
    return state, token


def tie_kernel(*refs):
    token, scratch = refs[-2:]
    scratch[...] = jnp.zeros_like(scratch)
    token[0] = 0


def tie(arrays, tokens=(), place=ANYWHERE):
    shape = jax.ShapeDtypeStruct if place is ANYWHERE else pltpu.HBM
    *arrays, token = pl.pallas_call(
        tie_kernel,
        out_shape=[shape(a.shape, a.dtype) for a in arrays] + [TOKEN],
        in_specs=[place] * len(arrays) + [SCALARS] * len(tokens),
        out_specs=[place] * len(arrays) + [SCALARS],
        input_output_aliases={i: i for i in range(len(arrays))},
        scratch_shapes=[pltpu.VMEM((8, BS), jnp.float32)],
        compiler_params=pltpu.CompilerParams(vmem_limit_bytes=1 << 20),
        cost_estimate=pl.CostEstimate(flops=0, bytes_accessed=0, transcendentals=0),
        name="tie",
    )(*(arrays if place is ANYWHERE else hbm(*arrays)), *tokens)
    return arrays, token


def witness(arrays, tokens=()):
    return pl.pallas_call(
        tie_kernel,
        out_shape=TOKEN,
        in_specs=[ANYWHERE] * len(arrays) + [SCALARS] * len(tokens),
        out_specs=SCALARS,
        scratch_shapes=[pltpu.VMEM((8, BS), jnp.float32)],
        compiler_params=pltpu.CompilerParams(vmem_limit_bytes=1 << 20),
        cost_estimate=pl.CostEstimate(flops=0, bytes_accessed=0, transcendentals=0),
        name="witness",
    )(*arrays, *tokens)


def pack_kernel(n, *refs):
    pieces, (out, bounce, into, leave) = refs[:n], refs[-4:]
    slots = [pl.ds(i * SA, SA) for i in range(n)]
    fill = [pltpu.make_async_copy(piece, bounce.at[rows], into.at[i]) for i, (piece, rows) in enumerate(zip(pieces, slots))]
    drain = [pltpu.make_async_copy(bounce.at[rows], out.at[rows], leave.at[i]) for i, rows in enumerate(slots)]
    for copy in fill:
        copy.start()
    for first, second in zip(fill, drain):
        first.wait()
        second.start()
    for copy in drain:
        copy.wait()


def pack(*pieces, later_than=()):
    n = len(pieces)
    return pl.pallas_call(
        lambda *refs: pack_kernel(n, *refs),
        out_shape=pltpu.HBM((n * SA, BS, BS), jnp.float32),
        in_specs=[IN_HBM] * (n + len(later_than)),
        out_specs=IN_HBM,
        scratch_shapes=[
            pltpu.VMEM((n * SA, BS, BS), jnp.float32),
            pltpu.SemaphoreType.DMA((n,)),
            pltpu.SemaphoreType.DMA((n,)),
        ],
        compiler_params=pltpu.CompilerParams(vmem_limit_bytes=(n + 1) << 20),
        cost_estimate=pl.CostEstimate(flops=0, bytes_accessed=0, transcendentals=0),
        name="pack",
    )(*hbm(*pieces, *later_than))


def shift(value, axis, by):
    size = lax.axis_size(axis)
    return lax.ppermute(value, axis, [(i, (i + by) % size) for i in range(size)])


def shift_apart(value, axis):
    size = lax.axis_size(axis)
    pairs = [(2 * i + core, (i + 1 - 2 * core) % size * 2 + core) for i in range(size) for core in range(2)]
    return lax.ppermute(value, (axis, "core"), pairs)


def order(left_index, right_index, target_index, count, row, layer, left_class):
    p = jnp.arange(PCAP, dtype=jnp.int32)
    away = (right_index // SA - row) % N_ROW
    kept = target_index // SCH == layer
    right_class = jnp.where((away <= 2) | (away >= 6), 0, jnp.where(away == 4, 2, 1))
    here = jnp.maximum(left_class, right_class)
    bins = jnp.where(here == 0, jnp.where(kept, 1, 0), jnp.where(kept, 5, 1 + here + (here == 2) * (target_index % SCH // (SCH // 2))))
    bins = jnp.where(p < count, bins, BINS)
    target = jnp.where(kept, 0, SCH) + target_index % SCH
    code = (left_index << 16) | (right_index << 8) | target
    same = bins[:, None] == bins[None, :]
    rank = jnp.sum(same & (p[None, :] < p[:, None]), axis=1, dtype=jnp.int32)
    held = jnp.sum(bins[None, :] == jnp.arange(BINS, dtype=jnp.int32)[:, None], axis=1, dtype=jnp.int32)
    groups = (held + UNROLL - 1) // UNROLL
    b = jnp.arange(BINS + 1, dtype=jnp.int32)
    bounds = jnp.sum(jnp.where(b[None, :BINS] < b[:, None], groups[None, :], 0), axis=1, dtype=jnp.int32)
    start = jnp.sum(jnp.where(bins[:, None] == b[None, :BINS], bounds[None, :BINS] * UNROLL, 0), axis=1)
    place = jnp.where(bins < BINS, start + rank, -1)
    slot = jnp.arange(LISTED, dtype=jnp.int32)
    hit = place[None, :] == slot[:, None]
    listed = SPARE + jnp.sum(jnp.where(hit, code[None, :] - SPARE, 0), axis=1, dtype=jnp.int32)
    return bounds, listed


def body(slab_blocks, factor_blocks, stack_left, stack_right, stack_target, stack_counts):
    row, layer = lax.axis_index("row"), lax.axis_index("layer")
    y, x, core = lax.axis_index("y"), lax.axis_index("x"), lax.axis_index("core")

    left_index = stack_left.reshape(-1)
    across_y = (left_index // (4 * SA) - y) % 4
    across_x = (left_index // (2 * SA) - x) % 2
    left_class = jnp.where((across_y == 2) | ((across_y != 0) & (across_x == 1)), 1, 0)
    bounds, listed = order(
        left_index,
        stack_right.reshape(-1),
        stack_target.reshape(-1),
        stack_counts.reshape(()),
        row,
        layer,
        left_class,
    )

    def left_at(dy, dx, dc, first=0):
        return (((y + dy) % 4 * 2 + (x + dx) % 2) * 2 + (core + dc) % 2) * SA + first

    def right_at(away, first=0):
        return (row + away) % N_ROW * SA + first

    own = slab_blocks.reshape(SA, BS, BS)
    mine = lax.all_to_all(factor_blocks.reshape(SA, BS, BS), ("y", "x", "core"), split_axis=0, concat_axis=0, tiled=True)

    first_places = [left_at(0, 0, 0), left_at(0, 0, 1), left_at(-1, 0, 0), left_at(1, 0, 0), left_at(0, 1, 0)]
    first_places += [left_at(-1, 0, 1), left_at(1, 0, 1), left_at(0, 1, 1)]
    first_places += [right_at(away) for away in (0, -1, 1, -2, 2)]
    second_places = [left_at(dy, dx, dc) for dy, dx in ((2, 0), (1, 1), (-1, 1), (2, 1)) for dc in range(2)]
    second_places += [right_at(-3), right_at(3)]
    third_places = [right_at(4)]
    starts = jnp.stack(first_places + second_places + third_places)
    second, third = len(first_places), len(first_places) + len(second_places)

    up1, down1 = shift(mine, "row", 1), shift(mine, "row", -1)
    own_c = shift(own, "core", 1)
    sent = pack(own, later_than=(shift(own[:1], "core", 1),))
    own_up, own_down, across = shift(sent, "y", 1), shift(sent, "y", -1), shift(sent, "x", 1)
    own_up_c, own_down_c, across_c = shift(own_up, "core", 1), shift(own_down, "core", 1), shift(across, "core", 1)
    z1 = witness((up1, down1))
    (own_up, own_down, across, own_c, own_up_c, own_down_c, across_c), _ = tie(
        (own_up, own_down, across, own_c, own_up_c, own_down_c, across_c), (z1,), IN_HBM
    )

    up2, down2 = shift(up1, "row", 1), shift(down1, "row", -1)
    own_far, across_down, across_up = shift(own_up, "y", 1), shift(across, "y", -1), shift(own_up, "x", 1)
    z2 = witness((up2, down2))
    (own_far, across_down, across_up), t2 = tie((own_far, across_down, across_up), (z2,), IN_HBM)

    up3, down3 = shift(up2, "row", 1), shift(down2, "row", -1)
    far = shift_apart(jnp.where(core == 0, across_up, across_down), "y")
    across_down_c = shift(across_down, "core", 1)
    lefts = [(1, a) for a in (own, own_c, own_up, own_down, across, own_up_c, own_down_c, across_c)]
    state, done = stage((0, 2), 0, lefts, [mine, up1, down1, up2, down2], bounds, listed, starts, flops=8 * 10**9, tokens=(t2,))

    (own_far,), _ = tie((own_far,), (done,), IN_HBM)
    own_far_c = shift(own_far, "core", 1)

    opposite = shift_apart(jnp.where(core == 0, up3, down3), "row")
    far_c, across_up_c = shift(far, "core", 1), shift(across_up, "core", 1)
    lefts = [(1, a) for a in (own_far, own_far_c, across_down, across_down_c, across_up, across_up_c, far, far_c)]
    state, done = stage((2, 3), second, lefts, [up3, down3], bounds, listed, starts, state, flops=1 * 10**7)

    state, _ = stage((3, 4), third, [], [opposite], bounds, listed, starts, state, place=ANYWHERE)
    arrived_low = shift(state[2][SCH : SCH + SCH // 2], "layer", 1)
    state, _ = stage((4, 5), 0, [], [], bounds, listed, starts, state)
    arrived_high = shift(state[2][SCH + SCH // 2 : 2 * SCH], "layer", 1)
    state, _ = stage((5, 6), 0, [], [], bounds, listed, starts, state, flops=10**10)
    summed = state[2][:SCH] + jnp.concatenate([arrived_low, arrived_high])
    return summed.reshape((1, 1, 1) + summed.shape)


def solution(mesh):
    fine = Mesh(mesh.devices.reshape(8, 4, 2, 2, 2), ("row", "y", "x", "core", "layer"))
    col = ("y", "x", "core")
    return jax.shard_map(
        body,
        mesh=fine,
        in_specs=(
            P("row", col, "layer", None, None, None),
            P("row", col, "layer", None, None, None, None),
            P("row", col, "layer", None),
            P("row", col, "layer", None),
            P("row", col, "layer", None),
            P("row", col, "layer"),
        ),
        out_specs=P("row", col, "layer", None, None, None),
        check_vma=False,
    )
```

```python
import jax
import jax.numpy as jnp
from jax import lax
from jax.experimental import pallas as pl
from jax.experimental.pallas import tpu as pltpu
from jax.sharding import Mesh
from jax.sharding import PartitionSpec as P

BS = 128
SA = 16
SCH = 16
N_ROW = 8
N_LEFT = 256
N_RIGHT = 128
PCAP = 512
UNROLL = 16
BINS = 6
LISTED = PCAP + BINS * UNROLL
SPARE = 2 * SCH

SCALARS = pl.BlockSpec(memory_space=pltpu.SMEM)
IN_HBM = pl.BlockSpec(memory_space=pltpu.HBM)
ANYWHERE = pl.BlockSpec(memory_space=pl.ANY)
VMEM = pl.BlockSpec(memory_space=pltpu.VMEM)
TOKEN = jax.ShapeDtypeStruct((1,), jnp.int32)
STATE = (
    pltpu.VMEM((N_LEFT, BS, BS), jnp.float32),
    pltpu.VMEM((N_RIGHT, BS, 2 * BS), jnp.bfloat16),
    pltpu.VMEM((2 * SCH + 1, BS, BS), jnp.float32),
)


def hbm(*arrays):
    return [pltpu.with_memory_space_constraint(a, pltpu.HBM) for a in arrays]


def vmem(*arrays):
    return [pltpu.with_memory_space_constraint(a, pltpu.VMEM) for a in arrays]


def split(block):
    high = block.astype(jnp.bfloat16)
    low = (block - high.astype(jnp.float32)).astype(jnp.bfloat16)
    return high, low


def block_product(left, right):
    lhs = jnp.concatenate(split(left), axis=1)
    rhs = jnp.concatenate([right, right], axis=0)
    both = lax.dot_general(lhs, rhs, (((1,), (0,)), ((), ())), preferred_element_type=jnp.float32)
    return both[:, :BS] + both[:, BS:]


def stage_kernel(bins, parts, n_rights, first, base, starts, bounds, listed, *refs):
    lefts, rights, refs = refs[: len(parts)], refs[len(parts) : len(parts) + n_rights], refs[len(parts) + n_rights :]
    if not first:
        refs = refs[3:]
    left, right, total, done, sems = refs
    copies = []
    for piece, n in zip(lefts, parts):
        length = piece.shape[0] // n
        for part in range(n):
            i = len(copies)
            source = piece.at[pl.ds(part * length, length)]
            copies.append(pltpu.make_async_copy(source, left.at[pl.ds(starts[base + i], length)], sems.at[i]))
    for copy in copies:
        copy.start()
    if first:
        total[...] = jnp.zeros_like(total)
    for i, piece in enumerate(rights):
        place = starts[base + len(copies) + i]

        def prepare(turn, carry, piece=piece, place=place):
            for step in range(8):
                block = turn * 8 + step
                high, low = split(piece[block])
                right[place + block, :, :BS] = high.T
                right[place + block, :, BS:] = low.T
            return carry

        lax.fori_loop(0, piece.shape[0] // 8, prepare, 0)
    for copy in copies:
        copy.wait()

    def accumulate(turn, carry):
        products, targets = [], []
        for step in range(UNROLL):
            code = listed[turn * UNROLL + step]
            targets.append(code & 255)
            products.append(block_product(left[code >> 16], right[(code >> 8) & 255]))
        for target, product in zip(targets, products):
            total[target] = total[target] + product
        return carry

    lax.fori_loop(bounds[bins[0]], bounds[bins[1]], accumulate, 0)
    done[0] = bounds[0]


def stage(bins, base, lefts, rights, bounds, listed, starts, state=None, flops=0, place=IN_HBM, tokens=()):
    parts, pieces = [n for n, _ in lefts], [a for _, a in lefts]
    n = len(tokens) + 3 + len(lefts) + len(rights)
    aliases = {} if state is None else {n + i: i for i in range(3)}
    *state, token = pl.pallas_call(
        lambda *refs: stage_kernel(bins, parts, len(rights), not aliases, base, *refs[len(tokens) :]),
        out_shape=[*STATE, TOKEN],
        in_specs=[SCALARS] * (len(tokens) + 3) + [place] * len(lefts) + [VMEM] * (len(rights) + len(aliases)),
        out_specs=[VMEM] * 3 + [SCALARS],
        input_output_aliases=aliases,
        scratch_shapes=[pltpu.SemaphoreType.DMA((max(1, sum(parts)),))],
        compiler_params=pltpu.CompilerParams(vmem_limit_bytes=10 << 20),
        cost_estimate=pl.CostEstimate(flops=flops, bytes_accessed=0, transcendentals=0),
        name="stage_" + "_".join(map(str, bins)),
    )(*tokens, starts, bounds, listed, *(hbm(*pieces) if place is IN_HBM else pieces), *vmem(*rights), *(state or ()))
    return state, token


def tie_kernel(*refs):
    token, scratch = refs[-2:]
    scratch[...] = jnp.zeros_like(scratch)
    token[0] = 0


def tie(arrays, tokens=(), place=ANYWHERE, flops=0):
    shape = jax.ShapeDtypeStruct if place is ANYWHERE else pltpu.HBM
    *arrays, token = pl.pallas_call(
        tie_kernel,
        out_shape=[shape(a.shape, a.dtype) for a in arrays] + [TOKEN],
        in_specs=[place] * len(arrays) + [SCALARS] * len(tokens),
        out_specs=[place] * len(arrays) + [SCALARS],
        input_output_aliases={i: i for i in range(len(arrays))},
        scratch_shapes=[pltpu.VMEM((8, BS), jnp.float32)],
        compiler_params=pltpu.CompilerParams(vmem_limit_bytes=1 << 20),
        cost_estimate=pl.CostEstimate(flops=flops, bytes_accessed=0, transcendentals=0),
        name="tie",
    )(*(arrays if place is ANYWHERE else hbm(*arrays)), *tokens)
    return arrays, token


def witness(arrays, tokens=()):
    return pl.pallas_call(
        tie_kernel,
        out_shape=TOKEN,
        in_specs=[ANYWHERE] * len(arrays) + [SCALARS] * len(tokens),
        out_specs=SCALARS,
        scratch_shapes=[pltpu.VMEM((8, BS), jnp.float32)],
        compiler_params=pltpu.CompilerParams(vmem_limit_bytes=1 << 20),
        cost_estimate=pl.CostEstimate(flops=0, bytes_accessed=0, transcendentals=0),
        name="witness",
    )(*arrays, *tokens)


def pack_kernel(n, *refs):
    pieces, (out, bounce, into, leave) = refs[:n], refs[-4:]
    slots = [pl.ds(i * SA, SA) for i in range(n)]
    fill = [pltpu.make_async_copy(piece, bounce.at[rows], into.at[i]) for i, (piece, rows) in enumerate(zip(pieces, slots))]
    drain = [pltpu.make_async_copy(bounce.at[rows], out.at[rows], leave.at[i]) for i, rows in enumerate(slots)]
    for copy in fill:
        copy.start()
    for first, second in zip(fill, drain):
        first.wait()
        second.start()
    for copy in drain:
        copy.wait()


def pack(*pieces, later_than=()):
    n = len(pieces)
    return pl.pallas_call(
        lambda *refs: pack_kernel(n, *refs),
        out_shape=pltpu.HBM((n * SA, BS, BS), jnp.float32),
        in_specs=[IN_HBM] * (n + len(later_than)),
        out_specs=IN_HBM,
        scratch_shapes=[
            pltpu.VMEM((n * SA, BS, BS), jnp.float32),
            pltpu.SemaphoreType.DMA((n,)),
            pltpu.SemaphoreType.DMA((n,)),
        ],
        compiler_params=pltpu.CompilerParams(vmem_limit_bytes=(n + 1) << 20),
        cost_estimate=pl.CostEstimate(flops=0, bytes_accessed=0, transcendentals=0),
        name="pack",
    )(*hbm(*pieces, *later_than))


def shift(value, axis, by):
    size = lax.axis_size(axis)
    return lax.ppermute(value, axis, [(i, (i + by) % size) for i in range(size)])


def shift_apart(value, axis):
    size = lax.axis_size(axis)
    pairs = [(2 * i + core, (i + 1 - 2 * core) % size * 2 + core) for i in range(size) for core in range(2)]
    return lax.ppermute(value, (axis, "core"), pairs)


def order(left_index, right_index, target_index, count, row, layer, left_class):
    p = jnp.arange(PCAP, dtype=jnp.int32)
    away = (right_index // SA - row) % N_ROW
    kept = target_index // SCH == layer
    right_class = jnp.where((away <= 2) | (away >= 6), 0, jnp.where(away == 4, 2, 1))
    here = jnp.maximum(left_class, right_class)
    bins = jnp.where(here == 0, jnp.where(kept, 1, 0), jnp.where(kept, 5, 1 + here + (here == 2) * (target_index % SCH // (SCH // 2))))
    bins = jnp.where(p < count, bins, BINS)
    target = jnp.where(kept, 0, SCH) + target_index % SCH
    code = (left_index << 16) | (right_index << 8) | target
    same = bins[:, None] == bins[None, :]
    rank = jnp.sum(same & (p[None, :] < p[:, None]), axis=1, dtype=jnp.int32)
    held = jnp.sum(bins[None, :] == jnp.arange(BINS, dtype=jnp.int32)[:, None], axis=1, dtype=jnp.int32)
    groups = (held + UNROLL - 1) // UNROLL
    b = jnp.arange(BINS + 1, dtype=jnp.int32)
    bounds = jnp.sum(jnp.where(b[None, :BINS] < b[:, None], groups[None, :], 0), axis=1, dtype=jnp.int32)
    start = jnp.sum(jnp.where(bins[:, None] == b[None, :BINS], bounds[None, :BINS] * UNROLL, 0), axis=1)
    place = jnp.where(bins < BINS, start + rank, -1)
    slot = jnp.arange(LISTED, dtype=jnp.int32)
    hit = place[None, :] == slot[:, None]
    listed = SPARE + jnp.sum(jnp.where(hit, code[None, :] - SPARE, 0), axis=1, dtype=jnp.int32)
    return bounds, listed


def body(slab_blocks, factor_blocks, stack_left, stack_right, stack_target, stack_counts):
    row, layer = lax.axis_index("row"), lax.axis_index("layer")
    y, x, core = lax.axis_index("y"), lax.axis_index("x"), lax.axis_index("core")

    left_index = stack_left.reshape(-1)
    across_y = (left_index // (4 * SA) - y) % 4
    across_x = (left_index // (2 * SA) - x) % 2
    left_class = jnp.where((across_y == 2) | ((across_y != 0) & (across_x == 1)), 1, 0)
    bounds, listed = order(
        left_index,
        stack_right.reshape(-1),
        stack_target.reshape(-1),
        stack_counts.reshape(()),
        row,
        layer,
        left_class,
    )

    def left_at(dy, dx, dc, first=0):
        return (((y + dy) % 4 * 2 + (x + dx) % 2) * 2 + (core + dc) % 2) * SA + first

    def right_at(away, first=0):
        return (row + away) % N_ROW * SA + first

    own = slab_blocks.reshape(SA, BS, BS)
    mine = lax.all_to_all(factor_blocks.reshape(SA, BS, BS), ("y", "x", "core"), split_axis=0, concat_axis=0, tiled=True)

    first_places = [left_at(0, 0, 0), left_at(0, 0, 1), left_at(-1, 0, 0), left_at(1, 0, 0), left_at(0, 1, 0)]
    first_places += [left_at(-1, 0, 1), left_at(1, 0, 1), left_at(0, 1, 1)]
    first_places += [right_at(away) for away in (0, -1, 1, -2, 2)]
    second_places = [left_at(dy, dx, dc) for dy, dx in ((2, 0), (1, 1), (-1, 1), (2, 1)) for dc in range(2)]
    second_places += [right_at(-3), right_at(3)]
    third_places = [right_at(4)]
    starts = jnp.stack(first_places + second_places + third_places)
    second, third = len(first_places), len(first_places) + len(second_places)

    own_c = shift(own, "core", 1)
    (mine,), _ = tie((mine,), (witness((own_c,)),), flops=10000000000)
    up1, down1 = shift(mine, "row", 1), shift(mine, "row", -1)
    sent = pack(own, later_than=(shift(own[:1], "core", 1),))
    own_up, own_down, across = shift(sent, "y", 1), shift(sent, "y", -1), shift(sent, "x", 1)
    own_up_c, own_down_c, across_c = shift(own_up, "core", 1), shift(own_down, "core", 1), shift(across, "core", 1)
    z1 = witness((up1, down1))
    (own_up, own_down, across, own_up_c, own_down_c, across_c), _ = tie(
        (own_up, own_down, across, own_up_c, own_down_c, across_c), (z1,), IN_HBM
    )

    up2, down2 = shift(up1, "row", 1), shift(down1, "row", -1)
    own_far, across_down, across_up = shift(own_up, "y", 1), shift(across, "y", -1), shift(own_up, "x", 1)
    z2 = witness((up2, down2))
    (own_far, across_down, across_up), t2 = tie((own_far, across_down, across_up), (z2,), IN_HBM)

    up3, down3 = shift(up2, "row", 1), shift(down2, "row", -1)
    far = shift_apart(jnp.where(core == 0, across_up, across_down), "y")
    across_down_c = shift(across_down, "core", 1)
    lefts = [(1, a) for a in (own, own_c, own_up, own_down, across, own_up_c, own_down_c, across_c)]
    state, done = stage((0, 2), 0, lefts, [mine, up1, down1, up2, down2], bounds, listed, starts, flops=8 * 10**9, tokens=(t2,))

    (own_far,), _ = tie((own_far,), (done,), IN_HBM)
    own_far_c = shift(own_far, "core", 1)

    opposite = shift_apart(jnp.where(core == 0, up3, down3), "row")
    far_c, across_up_c = shift(far, "core", 1), shift(across_up, "core", 1)
    lefts = [(1, a) for a in (own_far, own_far_c, across_down, across_down_c, across_up, across_up_c, far, far_c)]
    state, done = stage((2, 3), second, lefts, [up3, down3], bounds, listed, starts, state, flops=1 * 10**7)

    state, _ = stage((3, 4), third, [], [opposite], bounds, listed, starts, state, place=ANYWHERE)
    arrived_low = shift(state[2][SCH : SCH + SCH // 2], "layer", 1)
    state, _ = stage((4, 5), 0, [], [], bounds, listed, starts, state)
    arrived_high = shift(state[2][SCH + SCH // 2 : 2 * SCH], "layer", 1)
    state, _ = stage((5, 6), 0, [], [], bounds, listed, starts, state, flops=10**10)
    summed = state[2][:SCH] + jnp.concatenate([arrived_low, arrived_high])
    return summed.reshape((1, 1, 1) + summed.shape)


def solution(mesh):
    fine = Mesh(mesh.devices.reshape(8, 4, 2, 2, 2), ("row", "y", "x", "core", "layer"))
    col = ("y", "x", "core")
    return jax.shard_map(
        body,
        mesh=fine,
        in_specs=(
            P("row", col, "layer", None, None, None),
            P("row", col, "layer", None, None, None, None),
            P("row", col, "layer", None),
            P("row", col, "layer", None),
            P("row", col, "layer", None),
            P("row", col, "layer"),
        ),
        out_specs=P("row", col, "layer", None, None, None),
        check_vma=False,
    )
```

```python
import jax
import jax.numpy as jnp
from jax import lax
from jax.experimental import pallas as pl
from jax.experimental.pallas import tpu as pltpu
from jax.sharding import Mesh
from jax.sharding import PartitionSpec as P

BS = 128
SA = 16
SCH = 16
N_ROW = 8
N_LEFT = 256
N_RIGHT = 128
PCAP = 512
UNROLL = 16
BINS = 6
LISTED = PCAP + BINS * UNROLL
SPARE = 2 * SCH

SCALARS = pl.BlockSpec(memory_space=pltpu.SMEM)
IN_HBM = pl.BlockSpec(memory_space=pltpu.HBM)
ANYWHERE = pl.BlockSpec(memory_space=pl.ANY)
VMEM = pl.BlockSpec(memory_space=pltpu.VMEM)
TOKEN = jax.ShapeDtypeStruct((1,), jnp.int32)
STATE = (
    pltpu.VMEM((N_LEFT, BS, BS), jnp.float32),
    pltpu.VMEM((N_RIGHT, BS, 2 * BS), jnp.bfloat16),
    pltpu.VMEM((2 * SCH + 1, BS, BS), jnp.float32),
)


def hbm(*arrays):
    return [pltpu.with_memory_space_constraint(a, pltpu.HBM) for a in arrays]


def vmem(*arrays):
    return [pltpu.with_memory_space_constraint(a, pltpu.VMEM) for a in arrays]


def split(block):
    high = block.astype(jnp.bfloat16)
    low = (block - high.astype(jnp.float32)).astype(jnp.bfloat16)
    return high, low


def block_product(left, right):
    lhs = jnp.concatenate(split(left), axis=1)
    rhs = jnp.concatenate([right, right], axis=0)
    both = lax.dot_general(lhs, rhs, (((1,), (0,)), ((), ())), preferred_element_type=jnp.float32)
    return both[:, :BS] + both[:, BS:]


def stage_kernel(bins, parts, n_rights, first, base, starts, bounds, listed, *refs):
    lefts, rights, refs = refs[: len(parts)], refs[len(parts) : len(parts) + n_rights], refs[len(parts) + n_rights :]
    if not first:
        refs = refs[3:]
    left, right, total, done, sems = refs
    copies = []
    for piece, n in zip(lefts, parts):
        length = piece.shape[0] // n
        for part in range(n):
            i = len(copies)
            source = piece.at[pl.ds(part * length, length)]
            copies.append(pltpu.make_async_copy(source, left.at[pl.ds(starts[base + i], length)], sems.at[i]))
    for copy in copies:
        copy.start()
    if first:
        total[...] = jnp.zeros_like(total)
    for i, piece in enumerate(rights):
        place = starts[base + len(copies) + i]

        def prepare(turn, carry, piece=piece, place=place):
            for step in range(8):
                block = turn * 8 + step
                high, low = split(piece[block])
                right[place + block, :, :BS] = high.T
                right[place + block, :, BS:] = low.T
            return carry

        lax.fori_loop(0, piece.shape[0] // 8, prepare, 0)
    for copy in copies:
        copy.wait()

    def accumulate(turn, carry):
        products, targets = [], []
        for step in range(UNROLL):
            code = listed[turn * UNROLL + step]
            targets.append(code & 255)
            products.append(block_product(left[code >> 16], right[(code >> 8) & 255]))
        for target, product in zip(targets, products):
            total[target] = total[target] + product
        return carry

    lax.fori_loop(bounds[bins[0]], bounds[bins[1]], accumulate, 0)
    done[0] = bounds[0]


def stage(bins, base, lefts, rights, bounds, listed, starts, state=None, flops=0, place=IN_HBM, tokens=()):
    parts, pieces = [n for n, _ in lefts], [a for _, a in lefts]
    n = len(tokens) + 3 + len(lefts) + len(rights)
    aliases = {} if state is None else {n + i: i for i in range(3)}
    *state, token = pl.pallas_call(
        lambda *refs: stage_kernel(bins, parts, len(rights), not aliases, base, *refs[len(tokens) :]),
        out_shape=[*STATE, TOKEN],
        in_specs=[SCALARS] * (len(tokens) + 3) + [place] * len(lefts) + [VMEM] * (len(rights) + len(aliases)),
        out_specs=[VMEM] * 3 + [SCALARS],
        input_output_aliases=aliases,
        scratch_shapes=[pltpu.SemaphoreType.DMA((max(1, sum(parts)),))],
        compiler_params=pltpu.CompilerParams(vmem_limit_bytes=10 << 20),
        cost_estimate=pl.CostEstimate(flops=flops, bytes_accessed=0, transcendentals=0),
        name="stage_" + "_".join(map(str, bins)),
    )(*tokens, starts, bounds, listed, *(hbm(*pieces) if place is IN_HBM else pieces), *vmem(*rights), *(state or ()))
    return state, token


def tie_kernel(*refs):
    token, scratch = refs[-2:]
    scratch[...] = jnp.zeros_like(scratch)
    token[0] = 0


def tie(arrays, tokens=(), place=ANYWHERE, flops=0):
    shape = jax.ShapeDtypeStruct if place is ANYWHERE else pltpu.HBM
    *arrays, token = pl.pallas_call(
        tie_kernel,
        out_shape=[shape(a.shape, a.dtype) for a in arrays] + [TOKEN],
        in_specs=[place] * len(arrays) + [SCALARS] * len(tokens),
        out_specs=[place] * len(arrays) + [SCALARS],
        input_output_aliases={i: i for i in range(len(arrays))},
        scratch_shapes=[pltpu.VMEM((8, BS), jnp.float32)],
        compiler_params=pltpu.CompilerParams(vmem_limit_bytes=1 << 20),
        cost_estimate=pl.CostEstimate(flops=flops, bytes_accessed=0, transcendentals=0),
        name="tie",
    )(*(arrays if place is ANYWHERE else hbm(*arrays)), *tokens)
    return arrays, token


def witness(arrays, tokens=()):
    return pl.pallas_call(
        tie_kernel,
        out_shape=TOKEN,
        in_specs=[ANYWHERE] * len(arrays) + [SCALARS] * len(tokens),
        out_specs=SCALARS,
        scratch_shapes=[pltpu.VMEM((8, BS), jnp.float32)],
        compiler_params=pltpu.CompilerParams(vmem_limit_bytes=1 << 20),
        cost_estimate=pl.CostEstimate(flops=0, bytes_accessed=0, transcendentals=0),
        name="witness",
    )(*arrays, *tokens)


def pack_kernel(n, *refs):
    pieces, (out, bounce, into, leave) = refs[:n], refs[-4:]
    slots = [pl.ds(i * SA, SA) for i in range(n)]
    fill = [pltpu.make_async_copy(piece, bounce.at[rows], into.at[i]) for i, (piece, rows) in enumerate(zip(pieces, slots))]
    drain = [pltpu.make_async_copy(bounce.at[rows], out.at[rows], leave.at[i]) for i, rows in enumerate(slots)]
    for copy in fill:
        copy.start()
    for first, second in zip(fill, drain):
        first.wait()
        second.start()
    for copy in drain:
        copy.wait()


def pack(*pieces, later_than=()):
    n = len(pieces)
    return pl.pallas_call(
        lambda *refs: pack_kernel(n, *refs),
        out_shape=pltpu.HBM((n * SA, BS, BS), jnp.float32),
        in_specs=[IN_HBM] * (n + len(later_than)),
        out_specs=IN_HBM,
        scratch_shapes=[
            pltpu.VMEM((n * SA, BS, BS), jnp.float32),
            pltpu.SemaphoreType.DMA((n,)),
            pltpu.SemaphoreType.DMA((n,)),
        ],
        compiler_params=pltpu.CompilerParams(vmem_limit_bytes=(n + 1) << 20),
        cost_estimate=pl.CostEstimate(flops=0, bytes_accessed=0, transcendentals=0),
        name="pack",
    )(*hbm(*pieces, *later_than))


def shift(value, axis, by):
    size = lax.axis_size(axis)
    return lax.ppermute(value, axis, [(i, (i + by) % size) for i in range(size)])


def shift_apart(value, axis):
    size = lax.axis_size(axis)
    pairs = [(2 * i + core, (i + 1 - 2 * core) % size * 2 + core) for i in range(size) for core in range(2)]
    return lax.ppermute(value, (axis, "core"), pairs)


def order(left_index, right_index, target_index, count, row, layer, left_class):
    p = jnp.arange(PCAP, dtype=jnp.int32)
    away = (right_index // SA - row) % N_ROW
    kept = target_index // SCH == layer
    right_class = jnp.where((away <= 2) | (away >= 6), 0, jnp.where(away == 4, 2, 1))
    here = jnp.maximum(left_class, right_class)
    sent = jnp.where(here == 0, 0, 1 + here + (here == 2) * (target_index % SCH // (SCH // 2)))
    bins = jnp.where(kept, 5, sent)
    bins = jnp.where(p < count, bins, BINS)
    target = jnp.where(kept, 0, SCH) + target_index % SCH
    code = (left_index << 16) | (right_index << 8) | target
    same = bins[:, None] == bins[None, :]
    rank = jnp.sum(same & (p[None, :] < p[:, None]), axis=1, dtype=jnp.int32)
    held = jnp.sum(bins[None, :] == jnp.arange(BINS, dtype=jnp.int32)[:, None], axis=1, dtype=jnp.int32)
    groups = (held + UNROLL - 1) // UNROLL
    b = jnp.arange(BINS + 1, dtype=jnp.int32)
    bounds = jnp.sum(jnp.where(b[None, :BINS] < b[:, None], groups[None, :], 0), axis=1, dtype=jnp.int32)
    start = jnp.sum(jnp.where(bins[:, None] == b[None, :BINS], bounds[None, :BINS] * UNROLL, 0), axis=1)
    place = jnp.where(bins < BINS, start + rank, -1)
    slot = jnp.arange(LISTED, dtype=jnp.int32)
    hit = place[None, :] == slot[:, None]
    listed = SPARE + jnp.sum(jnp.where(hit, code[None, :] - SPARE, 0), axis=1, dtype=jnp.int32)
    return bounds, listed


def body(slab_blocks, factor_blocks, stack_left, stack_right, stack_target, stack_counts):
    row, layer = lax.axis_index("row"), lax.axis_index("layer")
    y, x, core = lax.axis_index("y"), lax.axis_index("x"), lax.axis_index("core")

    left_index = stack_left.reshape(-1)
    across_y = (left_index // (4 * SA) - y) % 4
    across_x = (left_index // (2 * SA) - x) % 2
    left_class = jnp.where((across_y == 2) | ((across_y != 0) & (across_x == 1)), 1, 0)
    bounds, listed = order(
        left_index,
        stack_right.reshape(-1),
        stack_target.reshape(-1),
        stack_counts.reshape(()),
        row,
        layer,
        left_class,
    )

    def left_at(dy, dx, dc, first=0):
        return (((y + dy) % 4 * 2 + (x + dx) % 2) * 2 + (core + dc) % 2) * SA + first

    def right_at(away, first=0):
        return (row + away) % N_ROW * SA + first

    own = slab_blocks.reshape(SA, BS, BS)
    mine = lax.all_to_all(factor_blocks.reshape(SA, BS, BS), ("y", "x", "core"), split_axis=0, concat_axis=0, tiled=True)

    first_places = [left_at(0, 0, 0), left_at(0, 0, 1), left_at(-1, 0, 0), left_at(1, 0, 0), left_at(0, 1, 0)]
    first_places += [left_at(-1, 0, 1), left_at(1, 0, 1), left_at(0, 1, 1)]
    first_places += [right_at(away) for away in (0, -1, 1, -2, 2)]
    second_places = [left_at(dy, dx, dc) for dy, dx in ((2, 0), (1, 1), (-1, 1), (2, 1)) for dc in range(2)]
    second_places += [right_at(-3), right_at(3)]
    third_places = [right_at(4)]
    starts = jnp.stack(first_places + second_places + third_places)
    second, third = len(first_places), len(first_places) + len(second_places)

    own_c = shift(own, "core", 1)
    (mine,), _ = tie((mine,), (witness((own_c,)),), flops=10000000000)
    up1, down1 = shift(mine, "row", 1), shift(mine, "row", -1)
    sent = pack(own, later_than=(shift(own[:1], "core", 1),))
    own_up, own_down, across = shift(sent, "y", 1), shift(sent, "y", -1), shift(sent, "x", 1)
    own_up_c, own_down_c, across_c = shift(own_up, "core", 1), shift(own_down, "core", 1), shift(across, "core", 1)
    z1 = witness((up1, down1))
    (own_up, own_down, across, own_up_c, own_down_c, across_c), _ = tie(
        (own_up, own_down, across, own_up_c, own_down_c, across_c), (z1,), IN_HBM
    )

    up2, down2 = shift(up1, "row", 1), shift(down1, "row", -1)
    own_far, across_down, across_up = shift(own_up, "y", 1), shift(across, "y", -1), shift(own_up, "x", 1)
    z2 = witness((up2, down2))
    (own_far, across_down, across_up), t2 = tie((own_far, across_down, across_up), (z2,), IN_HBM)

    up3, down3 = shift(up2, "row", 1), shift(down2, "row", -1)
    far = shift_apart(jnp.where(core == 0, across_up, across_down), "y")
    across_down_c = shift(across_down, "core", 1)
    lefts = [(1, a) for a in (own, own_c, own_up, own_down, across, own_up_c, own_down_c, across_c)]
    state, done = stage((0, 2), 0, lefts, [mine, up1, down1, up2, down2], bounds, listed, starts, flops=8 * 10**9, tokens=(t2,))

    (own_far,), _ = tie((own_far,), (done,), IN_HBM)
    own_far_c = shift(own_far, "core", 1)

    opposite = shift_apart(jnp.where(core == 0, up3, down3), "row")
    far_c, across_up_c = shift(far, "core", 1), shift(across_up, "core", 1)
    lefts = [(1, a) for a in (own_far, own_far_c, across_down, across_down_c, across_up, across_up_c, far, far_c)]
    state, done = stage((2, 3), second, lefts, [up3, down3], bounds, listed, starts, state, flops=1 * 10**7)

    state, _ = stage((3, 4), third, [], [opposite], bounds, listed, starts, state, place=ANYWHERE)
    arrived_low = shift(state[2][SCH : SCH + SCH // 2], "layer", 1)
    state, _ = stage((4, 5), 0, [], [], bounds, listed, starts, state)
    arrived_high = shift(state[2][SCH + SCH // 2 : 2 * SCH], "layer", 1)
    state, _ = stage((5, 6), 0, [], [], bounds, listed, starts, state, flops=10**10)
    summed = state[2][:SCH] + jnp.concatenate([arrived_low, arrived_high])
    return summed.reshape((1, 1, 1) + summed.shape)


def solution(mesh):
    fine = Mesh(mesh.devices.reshape(8, 4, 2, 2, 2), ("row", "y", "x", "core", "layer"))
    col = ("y", "x", "core")
    return jax.shard_map(
        body,
        mesh=fine,
        in_specs=(
            P("row", col, "layer", None, None, None),
            P("row", col, "layer", None, None, None, None),
            P("row", col, "layer", None),
            P("row", col, "layer", None),
            P("row", col, "layer", None),
            P("row", col, "layer"),
        ),
        out_specs=P("row", col, "layer", None, None, None),
        check_vma=False,
    )
```
